1024 devices in a mesh: tile: 128 (over y, z_lo, core), strip: 8 (over x, z_hi).
Axes of the slice: x: 4, y: 8, z: 16 (z_hi: 2, z_lo: 8; z = z_hi * 8 + z_lo), core: 2. Of those that a mesh axis runs over, the one named last changes fastest.
Arguments:
- fine_cotangent: float32 [70, 512, 4096], P(None, 'tile', 'strip'), may hold values from -6 to 6
- middle_cotangent: float32 [70, 256, 2048], P(None, 'tile', 'strip'), may hold values from -12 to 12
- coarse_cotangent: float32 [70, 128, 1024], P(None, 'tile', 'strip'), may hold values from -24 to 24
- fine_shift: float32 [70, 512, 4096], P(None, 'tile', 'strip'), may hold values from 0.5 to 2
- middle_shift: float32 [70, 256, 2048], P(None, 'tile', 'strip'), may hold values from 0.5 to 2
- coarse_shift: float32 [70, 128, 1024], P(None, 'tile', 'strip'), may hold values from 0.5 to 2
- lower_coupling: float32 [70], replicated, may hold values from 0.4 to 1
- upper_coupling: float32 [70], replicated, may hold values from 0.4 to 1
- seam_flip: int32 [128], replicated, may hold values from 0 to 1
Outputs:
- adjoint_field: float32 [70, 512, 4096], P(None, 'tile', 'strip')
The draws below stay inside these ranges and needn't reach their ends.
All inputs are finite; a program needn't handle non-finite values.
Results may differ from the reference program's by a relative error of at most 0.00002.
Values sent between devices are 32-bit elements; how exact they have to be, the bound alone decides.
No kernel may reach another device: no remote copies, remote signals or barrier semaphores. Data moves between devices by JAX's collectives and lax.ppermute only.
A program may use at most 128 MiB of HBM per device.

```python
import math
import jax
import jax.numpy as jnp

LEVELS = 70
NXF = 512
NYF = 4096
NXM = 256
NYM = 2048
NXC = 128
NYC = 1024
N_TILE = 128
N_STRIP = 8


def draw_fine_shift(key, part):
    key = jax.random.fold_in(key, 11)
    shape = (LEVELS, NXF, NYF)
    values = 0.5 * jnp.exp(jax.random.uniform(key, shape, jnp.float32) * math.log(4.0))
    return values.astype(jnp.float32)


def draw_middle_shift(key, part):
    key = jax.random.fold_in(key, 12)
    shape = (LEVELS, NXM, NYM)
    values = 0.5 * jnp.exp(jax.random.uniform(key, shape, jnp.float32) * math.log(4.0))
    return values.astype(jnp.float32)


def draw_coarse_shift(key, part):
    key = jax.random.fold_in(key, 13)
    shape = (LEVELS, NXC, NYC)
    values = 0.5 * jnp.exp(jax.random.uniform(key, shape, jnp.float32) * math.log(4.0))
    return values.astype(jnp.float32)


def draw_lower_coupling(key, part):
    key = jax.random.fold_in(key, 21)
    values = 0.4 * jnp.exp(jax.random.uniform(key, (LEVELS,), jnp.float32) * math.log(2.5))
    return values.astype(jnp.float32)


def draw_upper_coupling(key, part):
    key = jax.random.fold_in(key, 22)
    values = 0.4 * jnp.exp(jax.random.uniform(key, (LEVELS,), jnp.float32) * math.log(2.5))
    return values.astype(jnp.float32)


def with_ends(values, stream_key, least, largest):
    shape = values.shape
    place = [jax.random.randint(jax.random.fold_in(stream_key, axis), (), 0, shape[axis]) for axis in range(len(shape))]
    values = values.at[tuple(place)].set(least)
    longest = shape.index(max(shape))
    place[longest] = (place[longest] + 1) % shape[longest]
    return values.at[tuple(place)].set(largest)


def steps_of(key, shape, shards, least, high):
    factor_of, own = 1.0, jax.random.fold_in(key, 6)
    for dim, parts in shards:
        heights = jnp.exp(jax.random.uniform(jax.random.fold_in(own, dim), (parts,), jnp.float32, least / len(shards), high / len(shards)))
        factor_of = factor_of * jnp.repeat(heights, shape[dim] // parts).reshape([-1 if axis == dim else 1 for axis in range(len(shape))])
    return factor_of


def bell_draw(rng, dims, deviation, bound, shards=(), dtype=jnp.bfloat16):
    values = jax.random.normal(rng, dims, jnp.float32) * deviation
    if len(shards) > 0:
        values = steps_of(rng, dims, shards, -0.22, 0.18) * values
    return jnp.clip(values, min=-bound, max=bound).astype(dtype)


def setup_inputs(seed: int = 0) -> dict:
    key_of = jax.random.split(jax.random.key(seed), 10)
    return {
        "fine_cotangent": bell_draw(key_of[0], (LEVELS, NXF, NYF), 1.0, 6.0, ((1, 128), (2, 8)), jnp.float32),
        "middle_cotangent": bell_draw(key_of[1], (LEVELS, NXM, NYM), 2.0, 12.0, ((1, 128), (2, 8)), jnp.float32),
        "coarse_cotangent": bell_draw(key_of[2], (LEVELS, NXC, NYC), 4.0, 24.0, ((1, 128), (2, 8)), jnp.float32),
        "fine_shift": draw_fine_shift(jax.random.fold_in(key_of[9], 71), 0),
        "middle_shift": draw_middle_shift(jax.random.fold_in(key_of[9], 71), 0),
        "coarse_shift": draw_coarse_shift(jax.random.fold_in(key_of[9], 71), 0),
        "lower_coupling": draw_lower_coupling(jax.random.fold_in(key_of[9], 71), 0),
        "upper_coupling": draw_upper_coupling(jax.random.fold_in(key_of[9], 71), 0),
        "seam_flip": with_ends(jax.random.randint(key_of[8], (N_TILE,), 0, 2), jax.random.fold_in(key_of[8], 1), 0, 1).astype(jnp.int32),
    }


def transposed_solve(rhs, shift, lower_coupling, upper_coupling):
    depth = rhs.shape[0]
    shape_rest = rhs.shape[1:]
    flat_rhs = rhs.reshape(depth, -1)
    flat_shift = shift.reshape(depth, -1)
    zero_one = jnp.zeros((1,), jnp.float32)
    lower_terms = jnp.concatenate([zero_one, -upper_coupling[:-1]])
    upper_terms = jnp.concatenate([-lower_coupling[1:], zero_one])
    diagonal = (lower_coupling + upper_coupling)[:, None] + flat_shift
    factor = jnp.zeros(flat_rhs.shape[1:], jnp.float32)
    partial_value = jnp.zeros(flat_rhs.shape[1:], jnp.float32)
    factors = []
    partials = []
    for level in range(depth):
        pivot = diagonal[level] - lower_terms[level] * factor
        factor = upper_terms[level] / pivot
        partial_value = (flat_rhs[level] - lower_terms[level] * partial_value) / pivot
        factors.append(factor)
        partials.append(partial_value)
    solved = jnp.zeros(flat_rhs.shape[1:], jnp.float32)
    outputs = [None] * depth
    for level in range(depth - 1, -1, -1):
        solved = partials[level] - factors[level] * solved
        outputs[level] = solved
    return jnp.stack(outputs, axis=0).reshape((depth,) + shape_rest)


def spread_rows(field, seam_flip):
    depth, height, width = field.shape
    blocks = field.reshape(depth, N_TILE, height // N_TILE, N_STRIP, width // N_STRIP)
    last_rows = blocks[:, :, -1]
    first_rows = blocks[:, :, 0]
    flipped = (seam_flip == 1)[None, :, None, None]
    before_rows = jnp.roll(jnp.where(flipped, last_rows[..., ::-1], last_rows), 1, axis=1)
    after_rows = jnp.where(flipped, jnp.roll(first_rows[..., ::-1], -1, axis=1), jnp.roll(first_rows, -1, axis=1))
    upward_rows = jnp.concatenate([before_rows[:, :, None], blocks[:, :, :-1]], axis=2)
    downward_rows = jnp.concatenate([blocks[:, :, 1:], after_rows[:, :, None]], axis=2)
    even_rows = 0.375 * blocks + 0.125 * upward_rows
    odd_rows = 0.375 * blocks + 0.125 * downward_rows
    return jnp.stack([even_rows, odd_rows], axis=3).reshape(depth, 2 * height, width)


def spread_columns(field):
    depth, height, width = field.shape
    padded = jnp.pad(field, ((0, 0), (0, 0), (1, 1)))
    even_cols = 0.375 * field + 0.125 * padded[:, :, :-2]
    odd_cols = 0.375 * field + 0.125 * padded[:, :, 2:]
    return jnp.stack([even_cols, odd_cols], axis=-1).reshape(depth, height, 2 * width)


def reference(fine_cotangent, middle_cotangent, coarse_cotangent, fine_shift, middle_shift, coarse_shift, lower_coupling, upper_coupling, seam_flip):
    coarse_solved = transposed_solve(coarse_cotangent, coarse_shift, lower_coupling, upper_coupling)
    middle_rhs = middle_cotangent + spread_columns(spread_rows(coarse_solved, seam_flip))
    middle_solved = transposed_solve(middle_rhs, middle_shift, lower_coupling, upper_coupling)
    fine_rhs = fine_cotangent + spread_columns(spread_rows(middle_solved, seam_flip))
    return transposed_solve(fine_rhs, fine_shift, lower_coupling, upper_coupling)
```

```python
import functools

import jax
import jax.numpy as jnp
import ml_dtypes
import numpy as np
from jax import lax
from jax.experimental import pallas as pl
from jax.experimental.pallas import tpu as pltpu
from jax.sharding import PartitionSpec as P

LANES = 128
GROUP = 14
PACK_LIMIT = 60 * 1024 * 1024
EDGES = 6
BOTH = ("tile", "strip")
VMEM = pl.BlockSpec(memory_space=pltpu.VMEM)
SMEM = pl.BlockSpec(memory_space=pltpu.SMEM)
ANY = pl.BlockSpec(memory_space=pl.ANY)


def edge_lane(a, b, e):
    return ((a + 1) * 5 + b + 2) * EDGES + e


def edge_maps():
    halo = 96
    to_middle = np.zeros((2, 2, LANES, LANES))
    to_fine = np.zeros((2, 2, LANES, LANES))
    for before in (0, 1):
        for after in (0, 1):
            w1, w2 = to_middle[before, after], to_fine[before, after]

            def spread(a, r, b, j):
                other, flip = {(-1, 1): (0, before), (0, 0): (-1, before), (0, 1): (1, after), (1, 0): (0, after)}[a, r]
                return [(edge_lane(a, b, j), 0.375), (edge_lane(other, b, 1 - j if flip else j), 0.125)]

            def put(w, terms, scale, out):
                for lane, weight in terms:
                    w[lane, out] += scale * weight

            rows = [(-1, 1, before), (0, 0, 0), (0, 1, 0), (1, 0, after)]
            for i, (a, r, flip) in enumerate(rows):
                for b in (-1, 1):
                    out = edge_lane(a, b, 2 + 2 * r)
                    put(w1, spread(a, r, b, 0), 0.375, out)
                    put(w1, spread(a, r, b - 1, 1), 0.125, out)
                    put(w1, spread(a, r, b, 1), 0.375, out + 1)
                    put(w1, spread(a, r, b + 1, 0), 0.125, out + 1)
                put(w1, spread(a, r, -1, 1), 1.0, halo + 2 * i + (1 if flip else 0))
                put(w1, spread(a, r, 1, 0), 1.0, halo + 2 * i + (0 if flip else 1))

            def cell(row, side):
                a, r, flip = rows[row]
                last = (side == 0) != bool(flip)
                return edge_lane(a, -1 if side == 0 else 1, 2 + 2 * r + (1 if last else 0))

            for i, (main, other) in enumerate(((1, 0), (1, 2), (2, 1), (2, 3))):
                for side in (0, 1):
                    w2[cell(main, side), 2 * i + side] += 0.375
                    w2[cell(other, side), 2 * i + side] += 0.125
    both = np.stack([to_middle.reshape(4, LANES, LANES), to_fine.reshape(4, LANES, LANES)])
    return both.reshape(8, LANES, LANES).astype(ml_dtypes.bfloat16)


def column_map():
    u = np.zeros((2 * LANES, 2 * LANES))
    for j in range(LANES):
        u[j, 2 * j] += 0.375
        u[j, 2 * j + 1] += 0.375
        if j > 0:
            u[j - 1, 2 * j] += 0.125
        if j < LANES - 1:
            u[j + 1, 2 * j + 1] += 0.125
    u[LANES, 0] = 0.125
    u[LANES + 1, 2 * LANES - 1] = 0.125
    return u.astype(ml_dtypes.bfloat16)


def exact_dot(x, w):
    high = x.astype(jnp.bfloat16)
    rest = x - high.astype(jnp.float32)
    middle = rest.astype(jnp.bfloat16)
    low = (rest - middle.astype(jnp.float32)).astype(jnp.bfloat16)
    dot = functools.partial(jnp.dot, preferred_element_type=jnp.float32)
    return (dot(low, w) + dot(middle, w)) + dot(high, w)


def lanes_of(shape):
    return lax.broadcasted_iota(jnp.int32, shape, len(shape) - 1)


def tile_is_odd():
    return lax.axis_index("tile") % 2 == 1


def fetch(pad, refs, raw, sems):
    depth = refs[0].shape[0]
    sources = [(ref, 0, 0) for ref in refs[:2]]
    sources += [(ref, r, h) for ref in refs[2:] for r in range(2) for h in range(2)]
    copies = []
    for i, (ref, r, h) in enumerate(sources):
        source = ref.at[:, r, pl.ds(h * LANES, LANES)]
        copies.append(pltpu.make_async_copy(source, raw.at[pl.ds(i * pad, depth)], sems.at[i]))
    for copy in copies:
        copy.start()
    tail = jnp.zeros((pad - depth, LANES), jnp.float32)
    for i in range(len(sources)):
        raw[i * pad + depth : (i + 1) * pad, :] = tail
    for copy in copies:
        copy.wait()
    return [raw[i * pad : (i + 1) * pad, :] for i in range(len(sources))]


def put_rows(pad, target, planes, take_first):
    target[0:pad, :] = planes[0]
    target[pad : 2 * pad, :] = planes[1]
    for plane in range(2):
        for h in range(2):
            first, last = planes[2 + 4 * plane + h], planes[4 + 4 * plane + h]
            at = (2 + 2 * plane + h) * pad
            target[at : at + pad, :] = jnp.where(take_first, first, last)


def pack_kernel(pad, cc_ref, cs_ref, mc_ref, ms_ref, edge_ref, yrow_ref, xrow_ref, raw, sems):
    odd = tile_is_odd()
    planes = fetch(pad, (cc_ref, cs_ref, mc_ref, ms_ref), raw, sems)
    lane = lanes_of((pad, LANES))
    columns = jnp.zeros((pad, LANES), jnp.float32)
    for plane in range(2):
        m = planes[2 + 4 * plane : 6 + 4 * plane]
        cells = [(planes[plane], 0), (planes[plane], LANES - 1), (m[0], 0), (m[1], LANES - 1), (m[2], 0), (m[3], LANES - 1)]
        for e, (source, at) in enumerate(cells):
            out = plane * EDGES + e
            moved = pltpu.roll(source, (out - at) % LANES, 1) if out != at else source
            columns = jnp.where(lane == out, moved, columns)
    packed = columns[0:8]
    for i in range(1, pad // 8):
        packed = packed + pltpu.roll(columns[8 * i : 8 * i + 8], GROUP * i, 1)
    edge_ref[...] = packed
    for target, take_first in ((yrow_ref, jnp.logical_not(odd)), (xrow_ref, odd)):
        put_rows(pad, target, planes, take_first)
        target[6 * pad : 6 * pad + 8, :] = packed


def gather_kernel(pad, own_ref, y_ref, x_ref, out_ref):
    odd = tile_is_odd()
    from_x, from_y = x_ref[6 * pad : 6 * pad + 8, :], y_ref[6 * pad : 6 * pad + 8, :]
    out_ref[0:8, :] = jnp.where(odd, from_x, from_y)
    out_ref[8:16, :] = own_ref[...]
    out_ref[16:24, :] = jnp.where(odd, from_y, from_x)


def eliminate(depth, lo_ref, up_ref, stages):
    middle = depth // 2
    halves = (
        list(range(middle)),
        list(range(depth - 1, middle - 1, -1)),
    )
    before = [[None, None] for _ in stages]
    minor = [[None, None] for _ in stages]
    last = [[None, None] for _ in stages]
    for j in range(max(map(len, halves))):
        for side, levels in enumerate(halves):
            if j >= len(levels):
                continue
            k = levels[j]
            total = lo_ref[k] + up_ref[k]
            if j > 0:
                product = up_ref[k - 1] * lo_ref[k] if side == 0 else lo_ref[k + 1] * up_ref[k]
            toward = (lo_ref[k + 1] if side == 0 else up_ref[k - 1]) if 0 < k < depth - 1 or j == 0 else None
            for n, (shift_at, put_inverse, put_factor) in enumerate(stages):
                diagonal = shift_at(k) + total
                if j == 0:
                    here = diagonal
                    inverse = 1.0 / here
                elif j == 1:
                    here = diagonal * minor[n][side] - product
                    inverse = minor[n][side] / here
                else:
                    here = diagonal * minor[n][side] - product * before[n][side]
                    inverse = minor[n][side] / here
                before[n][side], minor[n][side] = minor[n][side], here
                last[n][side] = toward * inverse
                put_inverse(k, inverse)
                put_factor(k, last[n][side])
    for n, (_, _, put_factor) in enumerate(stages):
        put_factor(depth, 1.0 / (1.0 - last[n][0] * last[n][1]))


def solve(depth, lo_ref, up_ref, sets):
    middle = depth // 2
    top = [None] * len(sets)
    bottom = [None] * len(sets)
    for j in range(depth - middle):
        for n, (rhs, inverse, factor, put, get) in enumerate(sets):
            if j < middle:
                i = inverse(j)
                v = rhs(j) * i
                top[n] = v if j == 0 else v + (up_ref[j - 1] * i) * top[n]
                put(j, top[n])
            k = depth - 1 - j
            i = inverse(k)
            v = rhs(k) * i
            bottom[n] = v if j == 0 else v + (lo_ref[k + 1] * i) * bottom[n]
            if k > middle:
                put(k, bottom[n])
    for n, (rhs, inverse, factor, put, get) in enumerate(sets):
        bottom[n] = (bottom[n] + factor(middle) * top[n]) * factor(depth)
        top[n] = top[n] + factor(middle - 1) * bottom[n]
        put(middle, bottom[n])
        put(middle - 1, top[n])
    for j in range(1, depth - middle):
        for n, (rhs, inverse, factor, put, get) in enumerate(sets):
            k = middle - 1 - j
            if k >= 0:
                top[n] = get(k) + factor(k) * top[n]
                put(k, top[n])
            k = middle + j
            bottom[n] = get(k) + factor(k) * bottom[n]
            put(k, bottom[n])


def reader(ref, rows):
    return lambda k: ref[rows(k), :]


def writer(ref, rows):
    def put(k, v):
        ref[rows(k), :] = v

    return put


def plane_set(ref, ip, e, rows):
    return (reader(ref, rows), reader(ip, rows), reader(e, rows), writer(ref, rows), reader(ref, rows))


def block(pad, ref, i):
    return ref[i * pad : (i + 1) * pad, :]


def spaced(pad, count):
    return lambda k: pl.ds(k, count, stride=pad) if count > 1 else pl.ds(k, 1)


def prepare_rows(pad, depth, lo_ref, up_ref, ccot, cshift, mshift, cip, ce, mip, me, fine):
    c_rows, m_rows = spaced(pad, ccot.shape[0] // pad), spaced(pad, 4)
    eliminate(depth, lo_ref, up_ref, [
        (reader(cshift, c_rows), writer(cip, c_rows), writer(ce, c_rows)),
        (reader(mshift, m_rows), writer(mip, m_rows), writer(me, m_rows)),
    ] + fine)
    solve(depth, lo_ref, up_ref, [plane_set(ccot, cip, ce, c_rows)])
    tail = jnp.zeros((pad - depth, LANES), jnp.float32)
    for n in range(ccot.shape[0] // pad):
        ccot[n * pad + depth : (n + 1) * pad, :] = tail


def own_kernel(
    pad, lo_ref, up_ref, edge_ref, yown_ref, xown_ref, fs_ref,
    edge_out, ccot, mcot, mip, me, fip, fe,
    cshift, mshift, cip, ce,
):
    odd = tile_is_odd()
    edge_out[...] = edge_ref[...]
    ccot[...] = block(pad, xown_ref, 0)
    cshift[...] = block(pad, xown_ref, 1)
    for h in range(2):
        for i, target in ((2 + h, mcot), (4 + h, mshift)):
            in_x, in_y = block(pad, xown_ref, i), block(pad, yown_ref, i)
            target[h * pad : (1 + h) * pad, :] = jnp.where(odd, in_x, in_y)
            target[(2 + h) * pad : (3 + h) * pad, :] = jnp.where(odd, in_y, in_x)

    def put_fine(ref):
        def put(k, v):
            ref[k] = v

        return put

    fine = [(lambda k: fs_ref[k], put_fine(fip), put_fine(fe))]
    prepare_rows(pad, fs_ref.shape[0], lo_ref, up_ref, ccot, cshift, mshift, cip, ce, mip, me, fine)


def outer_kernel(
    pad, depth, flip_ref, lo_ref, up_ref, y_ref, x_ref,
    ccot, mcot, mip, me,
    cshift, mshift, cip, ce,
):
    t, tiles = lax.axis_index("tile"), lax.axis_size("tile")
    odd = tile_is_odd()
    back = (LANES - 1) - lanes_of((8, LANES))

    def reverse(x):
        return jnp.concatenate(
            [jnp.take_along_axis(x[8 * i : 8 * i + 8], back, axis=1) for i in range(pad // 8)], axis=0
        )

    for n in range(2):
        flip = flip_ref[lax.rem(t + tiles - 1, tiles) if n == 0 else t] == 1
        from_x = odd if n == 0 else jnp.logical_not(odd)
        plane = lambda i: jnp.where(from_x, block(pad, x_ref, i), block(pad, y_ref, i))
        for i, target in ((0, ccot), (1, cshift)):
            x = plane(i)
            target[n * pad : (n + 1) * pad, :] = jnp.where(flip, reverse(x), x)
        for i, target in ((2, mcot), (4, mshift)):
            x, y = plane(i), plane(i + 1)
            target[2 * n * pad : (2 * n + 1) * pad, :] = jnp.where(flip, reverse(y), x)
            target[(2 * n + 1) * pad : (2 * n + 2) * pad, :] = jnp.where(flip, reverse(x), y)
    prepare_rows(pad, depth, lo_ref, up_ref, ccot, cshift, mshift, cip, ce, mip, me, [])


def solve_kernel(
    pad, flip_ref, lo_ref, up_ref, c_own, m_own, ip_own, e_own, fip, fe, c_outer, m_outer, ip_outer, e_outer, fc_ref,
    own_ref, odd1_ref, odd_1_ref, even2_ref, even_2_ref, even_1_ref, even1_ref, odd2_ref, odd_2_ref, maps_ref, cols_ref,
    out_ref,
    ecot, eshift, eip, ee, mid, emid, xm, xf, fadd,
):
    depth = fc_ref.shape[0]
    t, s = lax.axis_index("tile"), lax.axis_index("strip")
    tiles, strips = lax.axis_size("tile"), lax.axis_size("strip")
    flips = flip_ref[lax.rem(t + tiles - 1, tiles)] * 2 + flip_ref[t]
    not_first, not_last = s > 0, s < strips - 1
    lane = lanes_of((pad, LANES))
    lane8 = lanes_of((8, LANES))
    tail = jnp.zeros((pad - depth, LANES), jnp.float32)

    packets = []
    for a in range(3):
        part = slice(8 * a, 8 * a + 8)
        packets += [
            (a - 1, -2, even2_ref[part, :] + odd2_ref[part, :]),
            (a - 1, -1, odd1_ref[part, :] + even1_ref[part, :]),
            (a - 1, 0, own_ref[part, :]),
            (a - 1, 1, odd_1_ref[part, :] + even_1_ref[part, :]),
            (a - 1, 2, even_2_ref[part, :] + odd_2_ref[part, :]),
        ]
    for i in range(pad // 8):
        cot = jnp.zeros((8, LANES), jnp.float32)
        shift = jnp.ones((8, LANES), jnp.float32)
        for a, b, packet in packets:
            at = edge_lane(a, b, 0)
            mask = (lane8 >= at) & (lane8 < at + EDGES)
            cot = jnp.where(mask, pltpu.roll(packet, (at - GROUP * i) % LANES, 1), cot)
            shift = jnp.where(mask, pltpu.roll(packet, (at - GROUP * i - EDGES) % LANES, 1), shift)
        ecot[8 * i : 8 * i + 8, :] = cot
        emid[8 * i : 8 * i + 8, :] = cot
        eshift[8 * i : 8 * i + 8, :] = shift

    one = lambda k: pl.ds(k, 1)
    eliminate(depth, lo_ref, up_ref, [(reader(eshift, one), writer(eip, one), writer(ee, one))])

    solve(depth, lo_ref, up_ref, [plane_set(ecot, eip, ee, one)])
    ecot[depth:, :] = tail
    c = [block(pad, c_outer, 0), c_own[...], block(pad, c_outer, 1)]
    edges = exact_dot(ecot[...], maps_ref[flips])
    for i, (main, other) in enumerate(((0, 1), (1, 0), (1, 2), (2, 1))):
        xm[i * pad : (i + 1) * pad, 0:LANES] = 0.375 * c[main] + 0.125 * c[other]
        sides = jnp.where(lane == 0, edges[:, 96 + 2 * i : 97 + 2 * i], 0.0)
        xm[i * pad : (i + 1) * pad, LANES:] = jnp.where(lane == 1, edges[:, 97 + 2 * i : 98 + 2 * i], sides)
    carried_rows = exact_dot(xm[...], cols_ref[...])
    place = (4, 0, 2, 6)
    for i in range(4):
        for h in range(2):
            at = place[i] + h
            raw = block(pad, m_own, at) if at < 4 else block(pad, m_outer, at - 4)
            mid[at * pad : (at + 1) * pad, :] = raw + block(pad, carried_rows, i)[:, h * LANES : (h + 1) * LANES]
    emid[...] = emid[...] + edges

    rows = spaced(pad, 4)
    outer = plane_set(mid, ip_outer, e_outer, lambda k: pl.ds(4 * pad + k, 4, stride=pad))
    outer = (outer[0], reader(ip_outer, rows), reader(e_outer, rows), outer[3], outer[4])
    solve(depth, lo_ref, up_ref, [plane_set(mid, ip_own, e_own, rows), outer, plane_set(emid, eip, ee, one)])
    for n in range(8):
        mid[n * pad + depth : (n + 1) * pad, :] = tail
    emid[depth:, :] = tail
    edges = exact_dot(emid[...], maps_ref[4 + flips])
    for i, (main, other) in enumerate(((1, 0), (1, 2), (2, 1), (2, 3))):
        halves = [
            0.375 * block(pad, mid, place[main] + h) + 0.125 * block(pad, mid, place[other] + h)
            for h in range(2)
        ]
        left = jnp.where(not_first, edges[:, 2 * i : 2 * i + 1], 0.0)
        right = jnp.where(not_last, edges[:, 2 * i + 1 : 2 * i + 2], 0.0)
        sides = ((left, halves[1][:, 0:1]), (halves[0][:, LANES - 1 :], right))
        for h in range(2):
            at = (2 * i + h) * pad
            xf[at : at + pad, 0:LANES] = halves[h]
            xf[at : at + pad, LANES:] = jnp.where(lane == 0, sides[h][0], jnp.where(lane == 1, sides[h][1], 0.0))
    carried_rows = exact_dot(xf[...], cols_ref[...])
    for i in range(4):
        for h in range(2):
            at = (2 * i + h) * pad
            for n in range(2):
                to = (4 * (2 * h + n) + i) * pad
                fadd[to : to + pad, :] = carried_rows[at : at + pad, n * LANES : (n + 1) * LANES]

    def fine_set(n):
        block = slice(n * LANES, (n + 1) * LANES)

        def put(k, v):
            out_ref[k, :, block] = v

        return (
            lambda k: fc_ref[k, :, block] + fadd[pl.ds(4 * n * pad + k, 4, stride=pad), :],
            lambda k: fip[k, :, block],
            lambda k: fe[k, :, block],
            put,
            lambda k: out_ref[k, :, block],
        )

    solve(depth, lo_ref, up_ref, [fine_set(n) for n in range(4)])


def moved(x, target):
    tiles, strips = lax.axis_size("tile"), lax.axis_size("strip")
    pairs = []
    for t in range(tiles):
        for s in range(strips):
            to = target(t, s)
            if to is not None and 0 <= to[1] < strips:
                pairs.append((t * strips + s, (to[0] % tiles) * strips + to[1]))
    return lax.ppermute(x, BOTH, pairs)


def on_device(fc, mc, cc, fs, ms, cs, lower, upper, seam_flip):
    depth = fc.shape[0]
    pad = (depth + 7) // 8 * 8
    f32 = jnp.float32
    array = lambda *shape: jax.ShapeDtypeStruct(shape, f32)
    scratch = lambda rows, width=LANES: pltpu.VMEM((rows * pad, width), f32)
    params = pltpu.CompilerParams(vmem_limit_bytes=24 * 1024 * 1024)
    fetched = [scratch(10), pltpu.SemaphoreType.DMA((10,))]
    fetching = pltpu.CompilerParams(vmem_limit_bytes=PACK_LIMIT)
    edge, yown, xown = pl.pallas_call(
        functools.partial(pack_kernel, pad),
        out_shape=(array(8, LANES), array(6 * pad + 8, LANES), array(6 * pad + 8, LANES)),
        in_specs=[ANY] * 4,
        out_specs=(VMEM,) * 3,
        scratch_shapes=[scratch(10), pltpu.SemaphoreType.DMA((10,))],
        compiler_params=pltpu.CompilerParams(vmem_limit_bytes=PACK_LIMIT),
    )(cc, cs, mc, ms)

    y = moved(yown, lambda t, s: (t + 1 if t % 2 else t - 1, s))
    x = moved(xown, lambda t, s: (t ^ 1, s))
    fine = array(*fc.shape)
    planes = lambda n: array(n * pad, LANES)
    edge, *own = pl.pallas_call(
        functools.partial(own_kernel, pad),
        out_shape=(array(8, LANES), planes(1), planes(4), planes(4), planes(4), fine, array(depth + 1, *fc.shape[1:])),
        in_specs=[SMEM] * 2 + [VMEM] * 4,
        out_specs=(VMEM,) * 7,
        scratch_shapes=[scratch(1), scratch(4), scratch(1), scratch(1)],
        compiler_params=params,
        cost_estimate=pl.CostEstimate(flops=20_000_000, bytes_accessed=4_000_000, transcendentals=0),
    )(lower, upper, edge, yown, xown, fs)
    columns = pl.pallas_call(
        functools.partial(gather_kernel, pad),
        out_shape=array(24, LANES),
        in_specs=[VMEM] * 3,
        out_specs=VMEM,
        compiler_params=params,
    )(edge, y, x)

    even = lambda step: moved(columns, lambda t, s: (t, s + step) if s % 2 == 0 else None)
    odd = lambda step: moved(columns, lambda t, s: (t, s + step) if s % 2 else None)
    strips = [odd(1), odd(-1), even(2), even(-2), even(-1), even(1), odd(2), odd(-2)]
    outer = pl.pallas_call(
        functools.partial(outer_kernel, pad, depth),
        out_shape=(planes(2), planes(4), planes(4), planes(4)),
        in_specs=[SMEM] * 3 + [VMEM] * 2,
        out_specs=(VMEM,) * 4,
        scratch_shapes=[scratch(2), scratch(4), scratch(2), scratch(2)],
        compiler_params=params,
        cost_estimate=pl.CostEstimate(flops=10_000_000, bytes_accessed=2_000_000, transcendentals=0),
    )(seam_flip, lower, upper, y, x)
    return pl.pallas_call(
        functools.partial(solve_kernel, pad),
        out_shape=fine,
        in_specs=[SMEM] * 3 + [VMEM] * 22,
        out_specs=VMEM,
        scratch_shapes=[scratch(1), scratch(1), scratch(1), scratch(1), scratch(8), scratch(1),
                        scratch(4, 2 * LANES), scratch(8, 2 * LANES), scratch(16)],
        compiler_params=params,
    )(seam_flip, lower, upper, *own, *outer, fc, columns, *strips,
      jnp.asarray(edge_maps()), jnp.asarray(column_map()))


def solution(mesh):
    field = P(None, "tile", "strip")
    return jax.shard_map(
        on_device, mesh=mesh, in_specs=(field,) * 6 + (P(),) * 3, out_specs=field, check_vma=False
    )
```

```python
import functools

import jax
import jax.numpy as jnp
import ml_dtypes
import numpy as np
from jax import lax
from jax.experimental import pallas as pl
from jax.experimental.pallas import tpu as pltpu
from jax.sharding import PartitionSpec as P

LANES = 128
GROUP = 14
PACK_LIMIT = 60 * 1024 * 1024
PLACE = (4, 0, 2, 6)
EDGES = 6
BOTH = ("tile", "strip")
VMEM = pl.BlockSpec(memory_space=pltpu.VMEM)
SMEM = pl.BlockSpec(memory_space=pltpu.SMEM)
ANY = pl.BlockSpec(memory_space=pl.ANY)


def edge_lane(a, b, e):
    return ((a + 1) * 5 + b + 2) * EDGES + e


def edge_maps():
    halo = 96
    to_middle = np.zeros((2, 2, LANES, LANES))
    to_fine = np.zeros((2, 2, LANES, LANES))
    for before in (0, 1):
        for after in (0, 1):
            w1, w2 = to_middle[before, after], to_fine[before, after]

            def spread(a, r, b, j):
                other, flip = {(-1, 1): (0, before), (0, 0): (-1, before), (0, 1): (1, after), (1, 0): (0, after)}[a, r]
                return [(edge_lane(a, b, j), 0.375), (edge_lane(other, b, 1 - j if flip else j), 0.125)]

            def put(w, terms, scale, out):
                for lane, weight in terms:
                    w[lane, out] += scale * weight

            rows = [(-1, 1, before), (0, 0, 0), (0, 1, 0), (1, 0, after)]
            for i, (a, r, flip) in enumerate(rows):
                for b in (-1, 1):
                    out = edge_lane(a, b, 2 + 2 * r)
                    put(w1, spread(a, r, b, 0), 0.375, out)
                    put(w1, spread(a, r, b - 1, 1), 0.125, out)
                    put(w1, spread(a, r, b, 1), 0.375, out + 1)
                    put(w1, spread(a, r, b + 1, 0), 0.125, out + 1)
                put(w1, spread(a, r, -1, 1), 1.0, halo + 2 * i + (1 if flip else 0))
                put(w1, spread(a, r, 1, 0), 1.0, halo + 2 * i + (0 if flip else 1))

            def cell(row, side):
                a, r, flip = rows[row]
                last = (side == 0) != bool(flip)
                return edge_lane(a, -1 if side == 0 else 1, 2 + 2 * r + (1 if last else 0))

            for i, (main, other) in enumerate(((1, 0), (1, 2), (2, 1), (2, 3))):
                for side in (0, 1):
                    w2[cell(main, side), 2 * i + side] += 0.375
                    w2[cell(other, side), 2 * i + side] += 0.125
    both = np.stack([to_middle.reshape(4, LANES, LANES), to_fine.reshape(4, LANES, LANES)])
    return both.reshape(8, LANES, LANES).astype(ml_dtypes.bfloat16)


def column_map():
    u = np.zeros((2 * LANES, 2 * LANES))
    for j in range(LANES):
        u[j, 2 * j] += 0.375
        u[j, 2 * j + 1] += 0.375
        if j > 0:
            u[j - 1, 2 * j] += 0.125
        if j < LANES - 1:
            u[j + 1, 2 * j + 1] += 0.125
    u[LANES, 0] = 0.125
    u[LANES + 1, 2 * LANES - 1] = 0.125
    return u.astype(ml_dtypes.bfloat16)


def exact_dot(x, w):
    high = x.astype(jnp.bfloat16)
    rest = x - high.astype(jnp.float32)
    middle = rest.astype(jnp.bfloat16)
    low = (rest - middle.astype(jnp.float32)).astype(jnp.bfloat16)
    dot = functools.partial(jnp.dot, preferred_element_type=jnp.float32)
    return (dot(low, w) + dot(middle, w)) + dot(high, w)


def lanes_of(shape):
    return lax.broadcasted_iota(jnp.int32, shape, len(shape) - 1)


def tile_is_odd():
    return lax.axis_index("tile") % 2 == 1


def fetch(pad, refs, raw, sems):
    depth = refs[0].shape[0]
    sources = [(ref, 0, 0) for ref in refs[:2]]
    sources += [(ref, r, h) for ref in refs[2:] for r in range(2) for h in range(2)]
    copies = []
    for i, (ref, r, h) in enumerate(sources):
        source = ref.at[:, r, pl.ds(h * LANES, LANES)]
        copies.append(pltpu.make_async_copy(source, raw.at[pl.ds(i * pad, depth)], sems.at[i]))
    for copy in copies:
        copy.start()
    tail = jnp.zeros((pad - depth, LANES), jnp.float32)
    for i in range(len(sources)):
        raw[i * pad + depth : (i + 1) * pad, :] = tail
    for copy in copies:
        copy.wait()
    return [raw[i * pad : (i + 1) * pad, :] for i in range(len(sources))]


def put_rows(pad, target, planes, take_first):
    target[0:pad, :] = planes[0]
    target[pad : 2 * pad, :] = planes[1]
    for plane in range(2):
        for h in range(2):
            first, last = planes[2 + 4 * plane + h], planes[4 + 4 * plane + h]
            at = (2 + 2 * plane + h) * pad
            target[at : at + pad, :] = jnp.where(take_first, first, last)


def pack_kernel(pad, cc_ref, cs_ref, mc_ref, ms_ref, edge_ref, yrow_ref, xrow_ref, raw, sems):
    odd = tile_is_odd()
    planes = fetch(pad, (cc_ref, cs_ref, mc_ref, ms_ref), raw, sems)
    lane = lanes_of((pad, LANES))
    columns = jnp.zeros((pad, LANES), jnp.float32)
    for plane in range(2):
        m = planes[2 + 4 * plane : 6 + 4 * plane]
        cells = [(planes[plane], 0), (planes[plane], LANES - 1), (m[0], 0), (m[1], LANES - 1), (m[2], 0), (m[3], LANES - 1)]
        for e, (source, at) in enumerate(cells):
            out = plane * EDGES + e
            moved = pltpu.roll(source, (out - at) % LANES, 1) if out != at else source
            columns = jnp.where(lane == out, moved, columns)
    packed = columns[0:8]
    for i in range(1, pad // 8):
        packed = packed + pltpu.roll(columns[8 * i : 8 * i + 8], GROUP * i, 1)
    edge_ref[...] = packed
    for target, take_first in ((yrow_ref, jnp.logical_not(odd)), (xrow_ref, odd)):
        put_rows(pad, target, planes, take_first)
        target[6 * pad : 6 * pad + 8, :] = packed


def gather_kernel(pad, own_ref, y_ref, x_ref, out_ref):
    odd = tile_is_odd()
    from_x, from_y = x_ref[6 * pad : 6 * pad + 8, :], y_ref[6 * pad : 6 * pad + 8, :]
    out_ref[0:8, :] = jnp.where(odd, from_x, from_y)
    out_ref[8:16, :] = own_ref[...]
    out_ref[16:24, :] = jnp.where(odd, from_y, from_x)


def eliminate(depth, lo_ref, up_ref, stages):
    middle = depth // 2
    halves = (
        list(range(middle)),
        list(range(depth - 1, middle - 1, -1)),
    )
    before = [[None, None] for _ in stages]
    minor = [[None, None] for _ in stages]
    last = [[None, None] for _ in stages]
    for j in range(max(map(len, halves))):
        for side, levels in enumerate(halves):
            if j >= len(levels):
                continue
            k = levels[j]
            total = lo_ref[k] + up_ref[k]
            if j > 0:
                product = up_ref[k - 1] * lo_ref[k] if side == 0 else lo_ref[k + 1] * up_ref[k]
            toward = (lo_ref[k + 1] if side == 0 else up_ref[k - 1]) if 0 < k < depth - 1 or j == 0 else None
            for n, (shift_at, put_inverse, put_factor) in enumerate(stages):
                diagonal = shift_at(k) + total
                if j == 0:
                    here = diagonal
                    inverse = 1.0 / here
                elif j == 1:
                    here = diagonal * minor[n][side] - product
                    inverse = minor[n][side] / here
                else:
                    here = diagonal * minor[n][side] - product * before[n][side]
                    inverse = minor[n][side] / here
                before[n][side], minor[n][side] = minor[n][side], here
                last[n][side] = toward * inverse
                put_inverse(k, inverse)
                put_factor(k, last[n][side])
    for n, (_, _, put_factor) in enumerate(stages):
        put_factor(depth, 1.0 / (1.0 - last[n][0] * last[n][1]))


def solve(depth, lo_ref, up_ref, sets):
    middle = depth // 2
    top = [None] * len(sets)
    bottom = [None] * len(sets)
    for j in range(depth - middle):
        for n, (rhs, inverse, factor, put, get) in enumerate(sets):
            if j < middle:
                i = inverse(j)
                v = rhs(j) * i
                top[n] = v if j == 0 else v + (up_ref[j - 1] * i) * top[n]
                put(j, top[n])
            k = depth - 1 - j
            i = inverse(k)
            v = rhs(k) * i
            bottom[n] = v if j == 0 else v + (lo_ref[k + 1] * i) * bottom[n]
            if k > middle:
                put(k, bottom[n])
    for n, (rhs, inverse, factor, put, get) in enumerate(sets):
        bottom[n] = (bottom[n] + factor(middle) * top[n]) * factor(depth)
        top[n] = top[n] + factor(middle - 1) * bottom[n]
        put(middle, bottom[n])
        put(middle - 1, top[n])
    for j in range(1, depth - middle):
        for n, (rhs, inverse, factor, put, get) in enumerate(sets):
            k = middle - 1 - j
            if k >= 0:
                top[n] = get(k) + factor(k) * top[n]
                put(k, top[n])
            k = middle + j
            bottom[n] = get(k) + factor(k) * bottom[n]
            put(k, bottom[n])


def reader(ref, rows):
    return lambda k: ref[rows(k), :]


def writer(ref, rows):
    def put(k, v):
        ref[rows(k), :] = v

    return put


def plane_set(ref, ip, e, rows):
    return (reader(ref, rows), reader(ip, rows), reader(e, rows), writer(ref, rows), reader(ref, rows))


def block(pad, ref, i):
    return ref[i * pad : (i + 1) * pad, :]


def spaced(pad, count):
    return lambda k: pl.ds(k, count, stride=pad) if count > 1 else pl.ds(k, 1)


def prepare_rows(pad, depth, lo_ref, up_ref, ccot, cshift, mshift, cip, ce, mip, me, fine):
    c_rows, m_rows = spaced(pad, ccot.shape[0] // pad), spaced(pad, 4)
    eliminate(depth, lo_ref, up_ref, [
        (reader(cshift, c_rows), writer(cip, c_rows), writer(ce, c_rows)),
        (reader(mshift, m_rows), writer(mip, m_rows), writer(me, m_rows)),
    ] + fine)
    solve(depth, lo_ref, up_ref, [plane_set(ccot, cip, ce, c_rows)])
    tail = jnp.zeros((pad - depth, LANES), jnp.float32)
    for n in range(ccot.shape[0] // pad):
        ccot[n * pad + depth : (n + 1) * pad, :] = tail


def own_kernel(
    pad, lo_ref, up_ref, edge_ref, yown_ref, xown_ref, fs_ref,
    edge_out, ccot, mcot, mip, me, fip, fe,
    cshift, mshift, cip, ce,
):
    odd = tile_is_odd()
    edge_out[...] = edge_ref[...]
    ccot[...] = block(pad, xown_ref, 0)
    cshift[...] = block(pad, xown_ref, 1)
    for h in range(2):
        for i, target in ((2 + h, mcot), (4 + h, mshift)):
            in_x, in_y = block(pad, xown_ref, i), block(pad, yown_ref, i)
            target[h * pad : (1 + h) * pad, :] = jnp.where(odd, in_x, in_y)
            target[(2 + h) * pad : (3 + h) * pad, :] = jnp.where(odd, in_y, in_x)

    def put_fine(ref):
        def put(k, v):
            ref[k] = v

        return put

    fine = [(lambda k: fs_ref[k], put_fine(fip), put_fine(fe))]
    prepare_rows(pad, fs_ref.shape[0], lo_ref, up_ref, ccot, cshift, mshift, cip, ce, mip, me, fine)


def first_half(
    pad, depth, flip_ref, lo_ref, up_ref, y_ref, x_ref, c_own, m_own, own_ref, sides, maps_ref, cols_ref,
    mid, emid, eip, ee, ip_outer, e_outer,
    ccot, cshift, mshift, cip, ce, ecot, eshift, xm,
):
    t, tiles = lax.axis_index("tile"), lax.axis_size("tile")
    odd = tile_is_odd()
    flips = flip_ref[lax.rem(t + tiles - 1, tiles)] * 2 + flip_ref[t]
    lane = lanes_of((pad, LANES))
    lane8 = lanes_of((8, LANES))
    back = (LANES - 1) - lane8
    tail = jnp.zeros((pad - depth, LANES), jnp.float32)

    def reverse(x):
        return jnp.concatenate(
            [jnp.take_along_axis(x[8 * i : 8 * i + 8], back, axis=1) for i in range(pad // 8)], axis=0
        )

    for n in range(2):
        flip = flip_ref[lax.rem(t + tiles - 1, tiles) if n == 0 else t] == 1
        from_x = odd if n == 0 else jnp.logical_not(odd)
        plane = lambda i: jnp.where(from_x, block(pad, x_ref, i), block(pad, y_ref, i))
        for i, target in ((0, ccot), (1, cshift)):
            x = plane(i)
            target[n * pad : (n + 1) * pad, :] = jnp.where(flip, reverse(x), x)
        for i, target, at in ((2, mid, 4 + 2 * n), (4, mshift, 2 * n)):
            x, y = plane(i), plane(i + 1)
            target[at * pad : (at + 1) * pad, :] = jnp.where(flip, reverse(y), x)
            target[(at + 1) * pad : (at + 2) * pad, :] = jnp.where(flip, reverse(x), y)

    packets = []
    for a in range(3):
        part = slice(8 * a, 8 * a + 8)
        packets += [(a - 1, b, ref[part, :]) for b, ref in ((0, own_ref),) + sides]
    for i in range(pad // 8):
        cot = jnp.zeros((8, LANES), jnp.float32)
        shift = jnp.ones((8, LANES), jnp.float32)
        for a, b, packet in packets:
            at = edge_lane(a, b, 0)
            mask = (lane8 >= at) & (lane8 < at + EDGES)
            cot = jnp.where(mask, pltpu.roll(packet, (at - GROUP * i) % LANES, 1), cot)
            shift = jnp.where(mask, pltpu.roll(packet, (at - GROUP * i - EDGES) % LANES, 1), shift)
        ecot[8 * i : 8 * i + 8, :] = cot
        emid[8 * i : 8 * i + 8, :] = cot
        eshift[8 * i : 8 * i + 8, :] = shift

    one, two, four = spaced(pad, 1), spaced(pad, 2), spaced(pad, 4)
    eliminate(depth, lo_ref, up_ref, [
        (reader(eshift, one), writer(eip, one), writer(ee, one)),
        (reader(cshift, two), writer(cip, two), writer(ce, two)),
        (reader(mshift, four), writer(ip_outer, four), writer(e_outer, four)),
    ])

    solve(depth, lo_ref, up_ref, [plane_set(ecot, eip, ee, one), plane_set(ccot, cip, ce, two)])
    ecot[depth:, :] = tail
    for n in range(2):
        ccot[n * pad + depth : (n + 1) * pad, :] = tail
    c = [block(pad, ccot, 0), c_own[...], block(pad, ccot, 1)]
    edges = exact_dot(ecot[...], maps_ref[flips])
    for i, (main, other) in enumerate(((0, 1), (1, 0), (1, 2), (2, 1))):
        xm[i * pad : (i + 1) * pad, 0:LANES] = 0.375 * c[main] + 0.125 * c[other]
        left = jnp.where(lane == 0, edges[:, 96 + 2 * i : 97 + 2 * i], 0.0)
        xm[i * pad : (i + 1) * pad, LANES:] = jnp.where(lane == 1, edges[:, 97 + 2 * i : 98 + 2 * i], left)
    carried_rows = exact_dot(xm[...], cols_ref[...])
    for i in range(4):
        for h in range(2):
            at = PLACE[i] + h
            raw = block(pad, m_own if at < 4 else mid, at)
            mid[at * pad : (at + 1) * pad, :] = raw + block(pad, carried_rows, i)[:, h * LANES : (h + 1) * LANES]
    emid[...] = emid[...] + edges


def even_kernel(
    pad, depth, flip_ref, lo_ref, up_ref, y_ref, x_ref, c_own, m_own, own_ref,
    even_2_ref, even2_ref, odd_1_ref, odd1_ref, maps_ref, cols_ref, *refs,
):
    sides = ((-2, even2_ref), (-1, odd1_ref), (1, odd_1_ref), (2, even_2_ref))

    @pl.when(lax.axis_index("strip") % 2 == 0)
    def _():
        first_half(
            pad, depth, flip_ref, lo_ref, up_ref, y_ref, x_ref, c_own, m_own, own_ref, sides, maps_ref, cols_ref, *refs
        )


def solve_kernel(
    pad, flip_ref, lo_ref, up_ref, y_ref, x_ref, c_own, m_own, own_ref,
    odd_2_ref, odd2_ref, even1_ref, even_1_ref, maps_ref, cols_ref,
    mid_ref, emid_ref, eip_ref, ee_ref, ip_outer_ref, e_outer_ref, ip_own, e_own, fip, fe, fc_ref,
    out_ref,
    mid, emid, eip, ee, ip_outer, e_outer,
    ccot, cshift, mshift, cip, ce, ecot, eshift, xm, xf, fadd,
):
    depth = fc_ref.shape[0]
    t, s = lax.axis_index("tile"), lax.axis_index("strip")
    tiles, strips = lax.axis_size("tile"), lax.axis_size("strip")
    flips = flip_ref[lax.rem(t + tiles - 1, tiles)] * 2 + flip_ref[t]
    not_first, not_last = s > 0, s < strips - 1
    lane = lanes_of((pad, LANES))
    tail = jnp.zeros((pad - depth, LANES), jnp.float32)

    @pl.when(s % 2 == 0)
    def _():
        for target, source in (
            (mid, mid_ref), (emid, emid_ref), (eip, eip_ref), (ee, ee_ref), (ip_outer, ip_outer_ref), (e_outer, e_outer_ref)
        ):
            target[...] = source[...]

    @pl.when(s % 2 == 1)
    def _():
        sides = ((-2, odd2_ref), (-1, even1_ref), (1, even_1_ref), (2, odd_2_ref))
        first_half(
            pad, depth, flip_ref, lo_ref, up_ref, y_ref, x_ref, c_own, m_own, own_ref, sides, maps_ref, cols_ref,
            mid, emid, eip, ee, ip_outer, e_outer,
            ccot, cshift, mshift, cip, ce, ecot, eshift, xm,
        )

    one, rows = spaced(pad, 1), spaced(pad, 4)
    outer = plane_set(mid, ip_outer, e_outer, lambda k: pl.ds(4 * pad + k, 4, stride=pad))
    outer = (outer[0], reader(ip_outer, rows), reader(e_outer, rows), outer[3], outer[4])
    solve(depth, lo_ref, up_ref, [plane_set(mid, ip_own, e_own, rows), outer, plane_set(emid, eip, ee, one)])
    for n in range(8):
        mid[n * pad + depth : (n + 1) * pad, :] = tail
    emid[depth:, :] = tail
    edges = exact_dot(emid[...], maps_ref[4 + flips])
    for i, (main, other) in enumerate(((1, 0), (1, 2), (2, 1), (2, 3))):
        halves = [
            0.375 * block(pad, mid, PLACE[main] + h) + 0.125 * block(pad, mid, PLACE[other] + h)
            for h in range(2)
        ]
        left = jnp.where(not_first, edges[:, 2 * i : 2 * i + 1], 0.0)
        right = jnp.where(not_last, edges[:, 2 * i + 1 : 2 * i + 2], 0.0)
        sides = ((left, halves[1][:, 0:1]), (halves[0][:, LANES - 1 :], right))
        for h in range(2):
            at = (2 * i + h) * pad
            xf[at : at + pad, 0:LANES] = halves[h]
            xf[at : at + pad, LANES:] = jnp.where(lane == 0, sides[h][0], jnp.where(lane == 1, sides[h][1], 0.0))
    carried_rows = exact_dot(xf[...], cols_ref[...])
    for i in range(4):
        for h in range(2):
            at = (2 * i + h) * pad
            for n in range(2):
                to = (4 * (2 * h + n) + i) * pad
                fadd[to : to + pad, :] = carried_rows[at : at + pad, n * LANES : (n + 1) * LANES]

    def fine_set(n):
        block = slice(n * LANES, (n + 1) * LANES)

        def put(k, v):
            out_ref[k, :, block] = v

        return (
            lambda k: fc_ref[k, :, block] + fadd[pl.ds(4 * n * pad + k, 4, stride=pad), :],
            lambda k: fip[k, :, block],
            lambda k: fe[k, :, block],
            put,
            lambda k: out_ref[k, :, block],
        )

    solve(depth, lo_ref, up_ref, [fine_set(n) for n in range(4)])


def moved(x, target):
    tiles, strips = lax.axis_size("tile"), lax.axis_size("strip")
    pairs = []
    for t in range(tiles):
        for s in range(strips):
            to = target(t, s)
            if to is not None and 0 <= to[1] < strips:
                pairs.append((t * strips + s, (to[0] % tiles) * strips + to[1]))
    return lax.ppermute(x, BOTH, pairs)


def on_device(fc, mc, cc, fs, ms, cs, lower, upper, seam_flip):
    depth = fc.shape[0]
    pad = (depth + 7) // 8 * 8
    f32 = jnp.float32
    array = lambda *shape: jax.ShapeDtypeStruct(shape, f32)
    scratch = lambda rows, width=LANES: pltpu.VMEM((rows * pad, width), f32)
    params = pltpu.CompilerParams(vmem_limit_bytes=24 * 1024 * 1024)
    fetched = [scratch(10), pltpu.SemaphoreType.DMA((10,))]
    fetching = pltpu.CompilerParams(vmem_limit_bytes=PACK_LIMIT)
    edge, yown, xown = pl.pallas_call(
        functools.partial(pack_kernel, pad),
        out_shape=(array(8, LANES), array(6 * pad + 8, LANES), array(6 * pad + 8, LANES)),
        in_specs=[ANY] * 4,
        out_specs=(VMEM,) * 3,
        scratch_shapes=[scratch(10), pltpu.SemaphoreType.DMA((10,))],
        compiler_params=pltpu.CompilerParams(vmem_limit_bytes=PACK_LIMIT),
    )(cc, cs, mc, ms)

    y = moved(yown, lambda t, s: (t + 1 if t % 2 else t - 1, s))
    x = moved(xown, lambda t, s: (t ^ 1, s))
    fine = array(*fc.shape)
    planes = lambda n: array(n * pad, LANES)
    edge, *own = pl.pallas_call(
        functools.partial(own_kernel, pad),
        out_shape=(array(8, LANES), planes(1), planes(4), planes(4), planes(4), fine, array(depth + 1, *fc.shape[1:])),
        in_specs=[SMEM] * 2 + [VMEM] * 4,
        out_specs=(VMEM,) * 7,
        scratch_shapes=[scratch(1), scratch(4), scratch(1), scratch(1)],
        compiler_params=params,
        cost_estimate=pl.CostEstimate(flops=20_000_000, bytes_accessed=4_000_000, transcendentals=0),
    )(lower, upper, edge, yown, xown, fs)
    columns = pl.pallas_call(
        functools.partial(gather_kernel, pad),
        out_shape=array(24, LANES),
        in_specs=[VMEM] * 3,
        out_specs=VMEM,
        compiler_params=params,
    )(edge, y, x)

    def send(x, parity, step):
        return moved(x, lambda t, s: (t, s + step) if s % 2 == parity else None)

    maps, cols = jnp.asarray(edge_maps()), jnp.asarray(column_map())
    shared = [scratch(2), scratch(2), scratch(4), scratch(2), scratch(2), scratch(1), scratch(1), scratch(4, 2 * LANES)]
    half_shapes = (8, 1, 1, 1, 4, 4)
    c_own, m_own, *own = own
    to_even = [send(columns, 0, -2), send(columns, 0, 2), send(columns, 1, -1), send(columns, 1, 1)]
    half = pl.pallas_call(
        functools.partial(even_kernel, pad, depth),
        out_shape=tuple(planes(n) for n in half_shapes),
        in_specs=[SMEM] * 3 + [VMEM] * 11,
        out_specs=(VMEM,) * 6,
        scratch_shapes=shared,
        compiler_params=params,
        cost_estimate=pl.CostEstimate(flops=10_000_000, bytes_accessed=2_000_000, transcendentals=0),
    )(seam_flip, lower, upper, y, x, c_own, m_own, columns, *to_even, maps, cols)
    late, half = lax.optimization_barrier((columns, half))
    to_odd = [send(late, 1, -2), send(late, 1, 2), send(late, 0, 1), send(late, 0, -1)]
    return pl.pallas_call(
        functools.partial(solve_kernel, pad),
        out_shape=fine,
        in_specs=[SMEM] * 3 + [VMEM] * 22,
        out_specs=VMEM,
        scratch_shapes=[scratch(n) for n in half_shapes] + shared + [scratch(8, 2 * LANES), scratch(16)],
        compiler_params=params,
    )(seam_flip, lower, upper, y, x, c_own, m_own, columns, *to_odd, maps, cols, *half, *own, fc)


def solution(mesh):
    field = P(None, "tile", "strip")
    return jax.shard_map(
        on_device, mesh=mesh, in_specs=(field,) * 6 + (P(),) * 3, out_specs=field, check_vma=False
    )
```

```python
import functools

import jax
import jax.numpy as jnp
import ml_dtypes
import numpy as np
from jax import lax
from jax.experimental import pallas as pl
from jax.experimental.pallas import tpu as pltpu
from jax.sharding import PartitionSpec as P

LANES = 128
GROUP = 14
PACK_LIMIT = 60 * 1024 * 1024
PLACE = (4, 0, 2, 6)
EDGES = 6
BOTH = ("tile", "strip")
VMEM = pl.BlockSpec(memory_space=pltpu.VMEM)
SMEM = pl.BlockSpec(memory_space=pltpu.SMEM)
ANY = pl.BlockSpec(memory_space=pl.ANY)


def edge_lane(a, b, e):
    return ((a + 1) * 5 + b + 2) * EDGES + e


def edge_maps():
    halo = 96
    to_middle = np.zeros((2, 2, LANES, LANES))
    to_fine = np.zeros((2, 2, LANES, LANES))
    for before in (0, 1):
        for after in (0, 1):
            w1, w2 = to_middle[before, after], to_fine[before, after]

            def spread(a, r, b, j):
                other, flip = {(-1, 1): (0, before), (0, 0): (-1, before), (0, 1): (1, after), (1, 0): (0, after)}[a, r]
                return [(edge_lane(a, b, j), 0.375), (edge_lane(other, b, 1 - j if flip else j), 0.125)]

            def put(w, terms, scale, out):
                for lane, weight in terms:
                    w[lane, out] += scale * weight

            rows = [(-1, 1, before), (0, 0, 0), (0, 1, 0), (1, 0, after)]
            for i, (a, r, flip) in enumerate(rows):
                for b in (-1, 1):
                    out = edge_lane(a, b, 2 + 2 * r)
                    put(w1, spread(a, r, b, 0), 0.375, out)
                    put(w1, spread(a, r, b - 1, 1), 0.125, out)
                    put(w1, spread(a, r, b, 1), 0.375, out + 1)
                    put(w1, spread(a, r, b + 1, 0), 0.125, out + 1)
                put(w1, spread(a, r, -1, 1), 1.0, halo + 2 * i + (1 if flip else 0))
                put(w1, spread(a, r, 1, 0), 1.0, halo + 2 * i + (0 if flip else 1))

            def cell(row, side):
                a, r, flip = rows[row]
                last = (side == 0) != bool(flip)
                return edge_lane(a, -1 if side == 0 else 1, 2 + 2 * r + (1 if last else 0))

            for i, (main, other) in enumerate(((1, 0), (1, 2), (2, 1), (2, 3))):
                for side in (0, 1):
                    w2[cell(main, side), 2 * i + side] += 0.375
                    w2[cell(other, side), 2 * i + side] += 0.125
    both = np.stack([to_middle.reshape(4, LANES, LANES), to_fine.reshape(4, LANES, LANES)])
    return both.reshape(8, LANES, LANES).astype(ml_dtypes.bfloat16)


def column_map():
    u = np.zeros((2 * LANES, 2 * LANES))
    for j in range(LANES):
        u[j, 2 * j] += 0.375
        u[j, 2 * j + 1] += 0.375
        if j > 0:
            u[j - 1, 2 * j] += 0.125
        if j < LANES - 1:
            u[j + 1, 2 * j + 1] += 0.125
    u[LANES, 0] = 0.125
    u[LANES + 1, 2 * LANES - 1] = 0.125
    return u.astype(ml_dtypes.bfloat16)


def exact_dot(x, w):
    high = x.astype(jnp.bfloat16)
    rest = x - high.astype(jnp.float32)
    middle = rest.astype(jnp.bfloat16)
    low = (rest - middle.astype(jnp.float32)).astype(jnp.bfloat16)
    dot = functools.partial(jnp.dot, preferred_element_type=jnp.float32)
    return (dot(low, w) + dot(middle, w)) + dot(high, w)


def lanes_of(shape):
    return lax.broadcasted_iota(jnp.int32, shape, len(shape) - 1)


def tile_is_odd():
    return lax.axis_index("tile") % 2 == 1


def fetch(pad, refs, raw, sems):
    depth = refs[0].shape[0]
    sources = [(ref, 0, 0) for ref in refs[:2]]
    sources += [(ref, r, h) for ref in refs[2:] for r in range(2) for h in range(2)]
    copies = []
    for i, (ref, r, h) in enumerate(sources):
        source = ref.at[:, r, pl.ds(h * LANES, LANES)]
        copies.append(pltpu.make_async_copy(source, raw.at[pl.ds(i * pad, depth)], sems.at[i]))
    for copy in copies:
        copy.start()
    tail = jnp.zeros((pad - depth, LANES), jnp.float32)
    for i in range(len(sources)):
        raw[i * pad + depth : (i + 1) * pad, :] = tail
    for copy in copies:
        copy.wait()
    return [raw[i * pad : (i + 1) * pad, :] for i in range(len(sources))]


def put_rows(pad, target, planes, take_first):
    target[0:pad, :] = planes[0]
    target[pad : 2 * pad, :] = planes[1]
    for plane in range(2):
        for h in range(2):
            first, last = planes[2 + 4 * plane + h], planes[4 + 4 * plane + h]
            at = (2 + 2 * plane + h) * pad
            target[at : at + pad, :] = jnp.where(take_first, first, last)


def pack_kernel(pad, cc_ref, cs_ref, mc_ref, ms_ref, edge_ref, yrow_ref, xrow_ref, raw, sems):
    odd = tile_is_odd()
    planes = fetch(pad, (cc_ref, cs_ref, mc_ref, ms_ref), raw, sems)
    lane = lanes_of((pad, LANES))
    columns = jnp.zeros((pad, LANES), jnp.float32)
    for plane in range(2):
        m = planes[2 + 4 * plane : 6 + 4 * plane]
        cells = [(planes[plane], 0), (planes[plane], LANES - 1), (m[0], 0), (m[1], LANES - 1), (m[2], 0), (m[3], LANES - 1)]
        for e, (source, at) in enumerate(cells):
            out = plane * EDGES + e
            moved = pltpu.roll(source, (out - at) % LANES, 1) if out != at else source
            columns = jnp.where(lane == out, moved, columns)
    packed = columns[0:8]
    for i in range(1, pad // 8):
        packed = packed + pltpu.roll(columns[8 * i : 8 * i + 8], GROUP * i, 1)
    edge_ref[...] = packed
    for target, take_first in ((yrow_ref, jnp.logical_not(odd)), (xrow_ref, odd)):
        put_rows(pad, target, planes, take_first)
        target[6 * pad : 6 * pad + 8, :] = packed


def gather_kernel(pad, own_ref, y_ref, x_ref, out_ref):
    odd = tile_is_odd()
    from_x, from_y = x_ref[6 * pad : 6 * pad + 8, :], y_ref[6 * pad : 6 * pad + 8, :]
    out_ref[0:8, :] = jnp.where(odd, from_x, from_y)
    out_ref[8:16, :] = own_ref[...]
    out_ref[16:24, :] = jnp.where(odd, from_y, from_x)


def eliminate(depth, lo_ref, up_ref, stages):
    middle = depth // 2
    halves = (
        list(range(middle)),
        list(range(depth - 1, middle - 1, -1)),
    )
    before = [[None, None] for _ in stages]
    minor = [[None, None] for _ in stages]
    last = [[None, None] for _ in stages]
    for j in range(max(map(len, halves))):
        for side, levels in enumerate(halves):
            if j >= len(levels):
                continue
            k = levels[j]
            total = lo_ref[k] + up_ref[k]
            if j > 0:
                product = up_ref[k - 1] * lo_ref[k] if side == 0 else lo_ref[k + 1] * up_ref[k]
            toward = (lo_ref[k + 1] if side == 0 else up_ref[k - 1]) if 0 < k < depth - 1 or j == 0 else None
            for n, (shift_at, put_inverse, put_factor) in enumerate(stages):
                diagonal = shift_at(k) + total
                if j == 0:
                    here = diagonal
                    inverse = 1.0 / here
                elif j == 1:
                    here = diagonal * minor[n][side] - product
                    inverse = minor[n][side] / here
                else:
                    here = diagonal * minor[n][side] - product * before[n][side]
                    inverse = minor[n][side] / here
                before[n][side], minor[n][side] = minor[n][side], here
                last[n][side] = toward * inverse
                put_inverse(k, inverse)
                put_factor(k, last[n][side])
    for n, (_, _, put_factor) in enumerate(stages):
        put_factor(depth, 1.0 / (1.0 - last[n][0] * last[n][1]))


def solve(depth, lo_ref, up_ref, sets):
    middle = depth // 2
    top = [None] * len(sets)
    bottom = [None] * len(sets)
    for j in range(depth - middle):
        for n, (rhs, inverse, factor, put, get) in enumerate(sets):
            if j < middle:
                i = inverse(j)
                v = rhs(j) * i
                top[n] = v if j == 0 else v + (up_ref[j - 1] * i) * top[n]
                put(j, top[n])
            k = depth - 1 - j
            i = inverse(k)
            v = rhs(k) * i
            bottom[n] = v if j == 0 else v + (lo_ref[k + 1] * i) * bottom[n]
            if k > middle:
                put(k, bottom[n])
    for n, (rhs, inverse, factor, put, get) in enumerate(sets):
        bottom[n] = (bottom[n] + factor(middle) * top[n]) * factor(depth)
        top[n] = top[n] + factor(middle - 1) * bottom[n]
        put(middle, bottom[n])
        put(middle - 1, top[n])
    for j in range(1, depth - middle):
        for n, (rhs, inverse, factor, put, get) in enumerate(sets):
            k = middle - 1 - j
            if k >= 0:
                top[n] = get(k) + factor(k) * top[n]
                put(k, top[n])
            k = middle + j
            bottom[n] = get(k) + factor(k) * bottom[n]
            put(k, bottom[n])


def reader(ref, rows):
    return lambda k: ref[rows(k), :]


def writer(ref, rows):
    def put(k, v):
        ref[rows(k), :] = v

    return put


def plane_set(ref, ip, e, rows):
    return (reader(ref, rows), reader(ip, rows), reader(e, rows), writer(ref, rows), reader(ref, rows))


def block(pad, ref, i):
    return ref[i * pad : (i + 1) * pad, :]


def spaced(pad, count):
    return lambda k: pl.ds(k, count, stride=pad) if count > 1 else pl.ds(k, 1)


def prepare_rows(pad, depth, lo_ref, up_ref, ccot, cshift, mshift, cip, ce, mip, me, fine):
    c_rows, m_rows = spaced(pad, ccot.shape[0] // pad), spaced(pad, 4)
    eliminate(depth, lo_ref, up_ref, [
        (reader(cshift, c_rows), writer(cip, c_rows), writer(ce, c_rows)),
        (reader(mshift, m_rows), writer(mip, m_rows), writer(me, m_rows)),
    ] + fine)
    solve(depth, lo_ref, up_ref, [plane_set(ccot, cip, ce, c_rows)])
    tail = jnp.zeros((pad - depth, LANES), jnp.float32)
    for n in range(ccot.shape[0] // pad):
        ccot[n * pad + depth : (n + 1) * pad, :] = tail


def own_kernel(
    pad, lo_ref, up_ref, edge_ref, yown_ref, xown_ref, fs_ref,
    edge_out, ccot, mcot, mip, me, fip, fe,
    cshift, mshift, cip, ce,
):
    odd = tile_is_odd()
    edge_out[...] = edge_ref[...]
    ccot[...] = block(pad, xown_ref, 0)
    cshift[...] = block(pad, xown_ref, 1)
    for h in range(2):
        for i, target in ((2 + h, mcot), (4 + h, mshift)):
            in_x, in_y = block(pad, xown_ref, i), block(pad, yown_ref, i)
            target[h * pad : (1 + h) * pad, :] = jnp.where(odd, in_x, in_y)
            target[(2 + h) * pad : (3 + h) * pad, :] = jnp.where(odd, in_y, in_x)

    def put_fine(ref):
        def put(k, v):
            ref[k] = v

        return put

    fine = [(lambda k: fs_ref[k], put_fine(fip), put_fine(fe))]
    prepare_rows(pad, fs_ref.shape[0], lo_ref, up_ref, ccot, cshift, mshift, cip, ce, mip, me, fine)


def first_half(
    pad, depth, flip_ref, lo_ref, up_ref, y_ref, x_ref, c_own, m_own, own_ref, sides, maps_ref, cols_ref,
    mid, emid, eip, ee, ip_outer, e_outer,
    ccot, cshift, mshift, cip, ce, ecot, eshift, xm,
):
    t, tiles = lax.axis_index("tile"), lax.axis_size("tile")
    odd = tile_is_odd()
    flips = flip_ref[lax.rem(t + tiles - 1, tiles)] * 2 + flip_ref[t]
    lane = lanes_of((pad, LANES))
    lane8 = lanes_of((8, LANES))
    back = (LANES - 1) - lane8
    tail = jnp.zeros((pad - depth, LANES), jnp.float32)

    def reverse(x):
        return jnp.concatenate(
            [jnp.take_along_axis(x[8 * i : 8 * i + 8], back, axis=1) for i in range(pad // 8)], axis=0
        )

    for n in range(2):
        flip = flip_ref[lax.rem(t + tiles - 1, tiles) if n == 0 else t] == 1
        from_x = odd if n == 0 else jnp.logical_not(odd)
        plane = lambda i: jnp.where(from_x, block(pad, x_ref, i), block(pad, y_ref, i))
        for i, target in ((0, ccot), (1, cshift)):
            x = plane(i)
            target[n * pad : (n + 1) * pad, :] = jnp.where(flip, reverse(x), x)
        for i, target, at in ((2, mid, 4 + 2 * n), (4, mshift, 2 * n)):
            x, y = plane(i), plane(i + 1)
            target[at * pad : (at + 1) * pad, :] = jnp.where(flip, reverse(y), x)
            target[(at + 1) * pad : (at + 2) * pad, :] = jnp.where(flip, reverse(x), y)

    packets = []
    for a in range(3):
        part = slice(8 * a, 8 * a + 8)
        packets += [(a - 1, b, ref[part, :]) for b, ref in ((0, own_ref),) + sides]
    for i in range(pad // 8):
        cot = jnp.zeros((8, LANES), jnp.float32)
        shift = jnp.ones((8, LANES), jnp.float32)
        for a, b, packet in packets:
            at = edge_lane(a, b, 0)
            mask = (lane8 >= at) & (lane8 < at + EDGES)
            cot = jnp.where(mask, pltpu.roll(packet, (at - GROUP * i) % LANES, 1), cot)
            shift = jnp.where(mask, pltpu.roll(packet, (at - GROUP * i - EDGES) % LANES, 1), shift)
        ecot[8 * i : 8 * i + 8, :] = cot
        emid[8 * i : 8 * i + 8, :] = cot
        eshift[8 * i : 8 * i + 8, :] = shift

    one, two, four = spaced(pad, 1), spaced(pad, 2), spaced(pad, 4)
    eliminate(depth, lo_ref, up_ref, [
        (reader(eshift, one), writer(eip, one), writer(ee, one)),
        (reader(cshift, two), writer(cip, two), writer(ce, two)),
        (reader(mshift, four), writer(ip_outer, four), writer(e_outer, four)),
    ])

    solve(depth, lo_ref, up_ref, [plane_set(ecot, eip, ee, one), plane_set(ccot, cip, ce, two)])
    ecot[depth:, :] = tail
    for n in range(2):
        ccot[n * pad + depth : (n + 1) * pad, :] = tail
    c = [block(pad, ccot, 0), c_own[...], block(pad, ccot, 1)]
    edges = exact_dot(ecot[...], maps_ref[flips])
    for i, (main, other) in enumerate(((0, 1), (1, 0), (1, 2), (2, 1))):
        xm[i * pad : (i + 1) * pad, 0:LANES] = 0.375 * c[main] + 0.125 * c[other]
        left = jnp.where(lane == 0, edges[:, 96 + 2 * i : 97 + 2 * i], 0.0)
        xm[i * pad : (i + 1) * pad, LANES:] = jnp.where(lane == 1, edges[:, 97 + 2 * i : 98 + 2 * i], left)
    carried_rows = exact_dot(xm[...], cols_ref[...])
    for i in range(4):
        for h in range(2):
            at = PLACE[i] + h
            raw = block(pad, m_own if at < 4 else mid, at)
            mid[at * pad : (at + 1) * pad, :] = raw + block(pad, carried_rows, i)[:, h * LANES : (h + 1) * LANES]
    emid[...] = emid[...] + edges


def even_kernel(
    pad, depth, flip_ref, lo_ref, up_ref, y_ref, x_ref, c_own, m_own, own_ref,
    even_2_ref, even2_ref, odd_1_ref, odd1_ref, maps_ref, cols_ref, low_ref, high_ref, *refs,
):
    sides = ((-2, even2_ref), (-1, odd1_ref), (1, odd_1_ref), (2, even_2_ref))

    @pl.when(lax.axis_index("strip") % 2 == 0)
    def _():
        for target, beyond in ((low_ref, odd_1_ref), (high_ref, odd1_ref)):
            target[0:24, :] = own_ref[...]
            target[24:48, :] = beyond[...]
        first_half(
            pad, depth, flip_ref, lo_ref, up_ref, y_ref, x_ref, c_own, m_own, own_ref, sides, maps_ref, cols_ref, *refs
        )


def solve_kernel(
    pad, flip_ref, lo_ref, up_ref, y_ref, x_ref, c_own, m_own, own_ref,
    even1_ref, even_1_ref, maps_ref, cols_ref,
    mid_ref, emid_ref, eip_ref, ee_ref, ip_outer_ref, e_outer_ref, ip_own, e_own, fip, fe, fc_ref,
    out_ref,
    mid, emid, eip, ee, ip_outer, e_outer,
    ccot, cshift, mshift, cip, ce, ecot, eshift, xm, xf, fadd,
):
    depth = fc_ref.shape[0]
    t, s = lax.axis_index("tile"), lax.axis_index("strip")
    tiles, strips = lax.axis_size("tile"), lax.axis_size("strip")
    flips = flip_ref[lax.rem(t + tiles - 1, tiles)] * 2 + flip_ref[t]
    not_first, not_last = s > 0, s < strips - 1
    lane = lanes_of((pad, LANES))
    tail = jnp.zeros((pad - depth, LANES), jnp.float32)

    @pl.when(s % 2 == 0)
    def _():
        for target, source in (
            (mid, mid_ref), (emid, emid_ref), (eip, eip_ref), (ee, ee_ref), (ip_outer, ip_outer_ref), (e_outer, e_outer_ref)
        ):
            target[...] = source[...]

    @pl.when(s % 2 == 1)
    def _():
        near, beyond = pl.ds(0, 24), pl.ds(24, 24)
        sides = (
            (-2, even1_ref.at[beyond]), (-1, even1_ref.at[near]), (1, even_1_ref.at[near]), (2, even_1_ref.at[beyond])
        )
        first_half(
            pad, depth, flip_ref, lo_ref, up_ref, y_ref, x_ref, c_own, m_own, own_ref, sides, maps_ref, cols_ref,
            mid, emid, eip, ee, ip_outer, e_outer,
            ccot, cshift, mshift, cip, ce, ecot, eshift, xm,
        )

    one, rows = spaced(pad, 1), spaced(pad, 4)
    outer = plane_set(mid, ip_outer, e_outer, lambda k: pl.ds(4 * pad + k, 4, stride=pad))
    outer = (outer[0], reader(ip_outer, rows), reader(e_outer, rows), outer[3], outer[4])
    solve(depth, lo_ref, up_ref, [plane_set(mid, ip_own, e_own, rows), outer, plane_set(emid, eip, ee, one)])
    for n in range(8):
        mid[n * pad + depth : (n + 1) * pad, :] = tail
    emid[depth:, :] = tail
    edges = exact_dot(emid[...], maps_ref[4 + flips])
    for i, (main, other) in enumerate(((1, 0), (1, 2), (2, 1), (2, 3))):
        halves = [
            0.375 * block(pad, mid, PLACE[main] + h) + 0.125 * block(pad, mid, PLACE[other] + h)
            for h in range(2)
        ]
        left = jnp.where(not_first, edges[:, 2 * i : 2 * i + 1], 0.0)
        right = jnp.where(not_last, edges[:, 2 * i + 1 : 2 * i + 2], 0.0)
        sides = ((left, halves[1][:, 0:1]), (halves[0][:, LANES - 1 :], right))
        for h in range(2):
            at = (2 * i + h) * pad
            xf[at : at + pad, 0:LANES] = halves[h]
            xf[at : at + pad, LANES:] = jnp.where(lane == 0, sides[h][0], jnp.where(lane == 1, sides[h][1], 0.0))
    carried_rows = exact_dot(xf[...], cols_ref[...])
    for i in range(4):
        for h in range(2):
            at = (2 * i + h) * pad
            for n in range(2):
                to = (4 * (2 * h + n) + i) * pad
                fadd[to : to + pad, :] = carried_rows[at : at + pad, n * LANES : (n + 1) * LANES]

    def fine_set(n):
        block = slice(n * LANES, (n + 1) * LANES)

        def put(k, v):
            out_ref[k, :, block] = v

        return (
            lambda k: fc_ref[k, :, block] + fadd[pl.ds(4 * n * pad + k, 4, stride=pad), :],
            lambda k: fip[k, :, block],
            lambda k: fe[k, :, block],
            put,
            lambda k: out_ref[k, :, block],
        )

    solve(depth, lo_ref, up_ref, [fine_set(n) for n in range(4)])


def moved(x, target):
    tiles, strips = lax.axis_size("tile"), lax.axis_size("strip")
    pairs = []
    for t in range(tiles):
        for s in range(strips):
            to = target(t, s)
            if to is not None and 0 <= to[1] < strips:
                pairs.append((t * strips + s, (to[0] % tiles) * strips + to[1]))
    return lax.ppermute(x, BOTH, pairs)


def on_device(fc, mc, cc, fs, ms, cs, lower, upper, seam_flip):
    depth = fc.shape[0]
    pad = (depth + 7) // 8 * 8
    f32 = jnp.float32
    array = lambda *shape: jax.ShapeDtypeStruct(shape, f32)
    scratch = lambda rows, width=LANES: pltpu.VMEM((rows * pad, width), f32)
    params = pltpu.CompilerParams(vmem_limit_bytes=24 * 1024 * 1024)
    fetched = [scratch(10), pltpu.SemaphoreType.DMA((10,))]
    fetching = pltpu.CompilerParams(vmem_limit_bytes=PACK_LIMIT)
    edge, yown, xown = pl.pallas_call(
        functools.partial(pack_kernel, pad),
        out_shape=(array(8, LANES), array(6 * pad + 8, LANES), array(6 * pad + 8, LANES)),
        in_specs=[ANY] * 4,
        out_specs=(VMEM,) * 3,
        scratch_shapes=[scratch(10), pltpu.SemaphoreType.DMA((10,))],
        compiler_params=pltpu.CompilerParams(vmem_limit_bytes=PACK_LIMIT),
    )(cc, cs, mc, ms)

    y = moved(yown, lambda t, s: (t + 1 if t % 2 else t - 1, s))
    x = moved(xown, lambda t, s: (t ^ 1, s))
    fine = array(*fc.shape)
    planes = lambda n: array(n * pad, LANES)
    edge, *own = pl.pallas_call(
        functools.partial(own_kernel, pad),
        out_shape=(array(8, LANES), planes(1), planes(4), planes(4), planes(4), fine, array(depth + 1, *fc.shape[1:])),
        in_specs=[SMEM] * 2 + [VMEM] * 4,
        out_specs=(VMEM,) * 7,
        scratch_shapes=[scratch(1), scratch(4), scratch(1), scratch(1)],
        compiler_params=params,
        cost_estimate=pl.CostEstimate(flops=20_000_000, bytes_accessed=4_000_000, transcendentals=0),
    )(lower, upper, edge, yown, xown, fs)
    columns = pl.pallas_call(
        functools.partial(gather_kernel, pad),
        out_shape=array(24, LANES),
        in_specs=[VMEM] * 3,
        out_specs=VMEM,
        compiler_params=params,
    )(edge, y, x)

    def send(x, parity, step):
        return moved(x, lambda t, s: (t, s + step) if s % 2 == parity else None)

    maps, cols = jnp.asarray(edge_maps()), jnp.asarray(column_map())
    shared = [scratch(2), scratch(2), scratch(4), scratch(2), scratch(2), scratch(1), scratch(1), scratch(4, 2 * LANES)]
    half_shapes = (8, 1, 1, 1, 4, 4)
    c_own, m_own, *own = own
    to_even = [send(columns, 0, -2), send(columns, 0, 2), send(columns, 1, -1), send(columns, 1, 1)]
    low, high, *half = pl.pallas_call(
        functools.partial(even_kernel, pad, depth),
        out_shape=(array(48, LANES),) * 2 + tuple(planes(n) for n in half_shapes),
        in_specs=[SMEM] * 3 + [VMEM] * 11,
        out_specs=(VMEM,) * 8,
        scratch_shapes=shared,
        compiler_params=params,
        cost_estimate=pl.CostEstimate(flops=10_000_000, bytes_accessed=2_000_000, transcendentals=0),
    )(seam_flip, lower, upper, y, x, c_own, m_own, columns, *to_even, maps, cols)
    to_odd = [send(high, 0, 1), send(low, 0, -1)]
    return pl.pallas_call(
        functools.partial(solve_kernel, pad),
        out_shape=fine,
        in_specs=[SMEM] * 3 + [VMEM] * 20,
        out_specs=VMEM,
        scratch_shapes=[scratch(n) for n in half_shapes] + shared + [scratch(8, 2 * LANES), scratch(16)],
        compiler_params=params,
    )(seam_flip, lower, upper, y, x, c_own, m_own, columns, *to_odd, maps, cols, *half, *own, fc)


def solution(mesh):
    field = P(None, "tile", "strip")
    return jax.shard_map(
        on_device, mesh=mesh, in_specs=(field,) * 6 + (P(),) * 3, out_specs=field, check_vma=False
    )
```
